32 devices in a mesh: groups: 2 (over y), ctx: 4 (over z), head: 2 (over x), sub: 2 (over core).
Axes of the slice: x: 2, y: 2, z: 4, core: 2. Of those that a mesh axis runs over, the one named last changes fastest.
Arguments:
- queries: bfloat16 [1024, 4096], P(('groups', 'ctx'), ('head', 'sub')), parts along dimension 0, may hold values from -40 to 40
- keys_values: bfloat16 [1024, 8, 128], P(('groups', 'ctx'), 'head'), parts along dimension 0, may hold values from -5 to 5
- sinks: float32 [64], P(('head', 'sub')), may hold values from 0 to 4
- out_weight: bfloat16 [4096, 2880], P(('head', 'sub')), may hold values from -0.09375 to 0.09375
- residual_in: bfloat16 [1024, 2880], P(('groups', 'ctx'), ('head', 'sub')), parts along dimension 0, may hold values from -96 to 96
- norm_gain: float32 [2880], replicated, may hold values from 0.5 to 1.5
- expert_ids: int32 [1024, 4], P(('groups', 'ctx')), parts along dimension 0, may hold values from 0 to 15, all different within a row; in each aligned block of 128 rows (0 to 127, 128 to 255, ...) at most 40 rows name the same one
- gate_weights: float32 [1024, 4], P(('groups', 'ctx')), parts along dimension 0, may hold values from 0.05 to 1
- gate_up: bfloat16 [16, 2880, 2, 2880], P('ctx', None, None, ('head', 'sub')), may hold values from -0.109375 to 0.109375
- down_weight: bfloat16 [16, 2880, 2880], P('ctx', None, ('head', 'sub')), may hold values from -0.109375 to 0.109375
Outputs:
- block_out: bfloat16 [1024, 2880], P(('groups', 'ctx'), ('head', 'sub')), parts along dimension 0
The draws below stay inside these ranges and needn't reach their ends.
There are 2 independent parts, one for each index of `groups`. The reference program is written for one: setup_inputs(seed, part) draws one part's arguments, and reference() takes and returns one part's arrays. A program takes and returns all parts, laid end to end along the dimension named above; an argument that names none is the same for every part. Nothing has to cross between parts.
Inputs may be any that keep to these rules, and one draw needn't show every extreme that they name: `expert_ids`: each row names 4 different experts; among the 128 rows of one index of ctx no expert is named by more than 40 rows, a bound that some block reaches.
All inputs are finite; a program needn't handle non-finite values.
Results may differ from the reference program's by a relative error of at most 0.015.
Values may be sent and summed in bfloat16 or wider, within the bound.
A program may use at most 192 MiB of HBM per device.

```python
import math
import jax
import jax.numpy as jnp
import numpy as np
from jax import lax

D = 2880
HEADS = 64
KV_HEADS = 8
HD = 64
WIN = 128
FF = 2880
EXPERTS = 16
TOP = 4
TOK_DEV = 128
TOKENS = 512
CAP = 40
SPLITS = 4
N_CTX = 4


def draw_queries(key, part):
    key = jax.random.fold_in(key, 7)
    normal_part = jax.random.truncated_normal(key, -5.0, 5.0, (TOKENS, HEADS * HD), jnp.float32)
    return normal_part.astype(jnp.bfloat16)


def draw_keys_values(key, part):
    key = jax.random.fold_in(key, 11)
    normal_part = jax.random.truncated_normal(key, -5.0, 5.0, (TOKENS, KV_HEADS, 2 * HD), jnp.float32)
    return normal_part.astype(jnp.bfloat16)


def draw_residual_in(key, part):
    key = jax.random.fold_in(key, 5)
    first = jax.random.fold_in(key, 0)
    values = jax.random.truncated_normal(first, -6.0, 6.0, (TOKENS, D), jnp.float32)
    return values.astype(jnp.bfloat16)


def shard_levels(own_key, shape, pieces, least, high):
    factor_of = 1.0
    for dim, parts in pieces:
        heights = jax.random.uniform(jax.random.fold_in(jax.random.fold_in(own_key, 6), dim), (parts,), jnp.float32, least / len(pieces), high / len(pieces))
        factor_of = factor_of * jnp.repeat(jnp.exp(heights), shape[dim] // parts).reshape((-1,) + (1,) * (len(shape) - 1 - dim))
    return factor_of


def routed_block(own_key, own, number, rows, count, top, reach, slope):
    order = jax.random.permutation(own_key, count)
    crowded, ordinary = portions_of(count, rows * top, reach, slope, True), portions_of(count, rows * top, reach, slope, False)
    places = jnp.arange(count)

    def named(tallies, turn):
        used = int((tallies > 0).sum())
        fixed = max(1, used // 4)
        passed = fixed + (places - fixed + turn * (used - fixed)) % max(1, count - fixed)
        return jnp.zeros((count,), jnp.int32).at[order[jnp.where(places < fixed, places, passed)]].set(jnp.asarray(tallies, jnp.int32))

    tallies = jnp.where(number % 4 == 0, named(crowded, number // 4), named(ordinary, number - number // 4 - 1))
    mixed = jax.random.permutation(jax.random.fold_in(own, 3), count)
    source_of, taker = mixed[0:count // 2 * 2:2], mixed[1:count // 2 * 2:2]
    margin = jnp.minimum(tallies[source_of] - 1, reach - tallies[taker]) // 2
    margin = jnp.where((source_of == order[0]) | (taker == order[0]) | (tallies[taker] == 0), 0, jnp.maximum(margin, 0))
    passed = jax.random.randint(jax.random.fold_in(own, 4), (count // 2,), 0, 1 << 20) % (margin + 1)
    tallies = tallies.at[source_of].add(-passed).at[taker].add(passed)
    members = jnp.searchsorted(jnp.cumsum(tallies), jnp.arange(rows * top), side="right").astype(jnp.int32)
    listing = members.reshape(top, rows).T
    listing = listing[jax.random.permutation(jax.random.fold_in(own, 1), rows)]
    turn = jax.random.randint(jax.random.fold_in(own, 2), (rows, 1), 0, top)
    return jnp.take_along_axis(listing, (jnp.arange(top)[None, :] + turn) % top, axis=1)


def portions_of(amount, total, bound, lean, full):
    loads = [(1 << 20) // math.isqrt(standing ** lean) + 1 for standing in range(1, amount + 1)]
    largest = bound if full else min(bound, max(-(-total // amount), total * loads[0] // sum(loads)))
    least = 1 if total - largest >= amount - 1 else 0
    holding, rest = [largest] + [least] * (amount - 1), total - largest - least * (amount - 1)
    while rest > 0:
        candidates = [i for i in range(1, amount) if holding[i] < largest] or [i for i in range(1, amount) if holding[i] < bound]
        mass, budget = sum([loads[i] for i in candidates]), rest
        for i in candidates:
            extra = min(bound - holding[i], max(1, budget * loads[i] // mass), rest)
            holding[i] = holding[i] + extra
            rest = rest - extra
    return np.array(holding)


def bell_draw(rng, shape, scale, limit, cuts=(), kind=jnp.bfloat16):
    values = jax.random.normal(rng, shape, jnp.float32) * scale
    if len(cuts) > 0:
        values = shard_levels(rng, shape, cuts, -0.22, 0.18) * values
    return jnp.clip(values, min=-limit, max=limit).astype(kind)


def setup_inputs(seed: int = 0, part: int = 0) -> dict:
    key_of = jax.random.split(jax.random.key(seed), 11)
    part_keys = jax.random.split(jax.random.fold_in(key_of[10], part), 11)
    queries = draw_queries(jax.random.fold_in(jax.random.fold_in(key_of[10], part), 71), part)
    keys_values = draw_keys_values(jax.random.fold_in(jax.random.fold_in(key_of[10], part), 71), part)
    sinks = jnp.clip(4.0 * jax.random.uniform(key_of[2], (HEADS,), jnp.float32) ** shard_levels(key_of[2], (HEADS,), ((0, 4),), -0.2, 0.2), 0.0, 4.0)
    out_weight = bell_draw(key_of[3], (HEADS * HD, D), (HEADS * HD) ** -0.5, 0.09375, ((0, 4),))
    residual_in = draw_residual_in(jax.random.fold_in(jax.random.fold_in(key_of[10], part), 71), part)
    norm_gain = jnp.clip(1.0 + 0.1 * jax.random.normal(key_of[5], (D,), jnp.float32), 0.5, 1.5)
    expert_ids_keys = jax.random.split(jax.random.fold_in(part_keys[6], 1), TOKENS // TOK_DEV)
    expert_ids_turns = jax.random.permutation(jax.random.fold_in(part_keys[6], 3), TOKENS // TOK_DEV)
    expert_ids = jax.vmap(lambda own, number: routed_block(jax.random.fold_in(part_keys[6], 2), own, number, TOK_DEV, EXPERTS, TOP, CAP, 2))(expert_ids_keys, expert_ids_turns).reshape((TOKENS, TOP))
    gate_weights = jnp.clip(jnp.exp(math.log(1.0) - 2.9957323 * jax.random.uniform(part_keys[7], (TOKENS, TOP), jnp.float32) ** shard_levels(part_keys[7], (TOKENS, TOP), ((0, 4),), -0.2, 0.2)), 0.05, 1.0)
    gate_up = bell_draw(key_of[8], (EXPERTS, D, 2, FF), D ** -0.5, 0.109375, ((0, 4), (3, 4)))
    down_weight = bell_draw(key_of[9], (EXPERTS, D, FF), FF ** -0.5, 0.109375, ((0, 4), (2, 4)))
    return {"queries": queries, "keys_values": keys_values, "sinks": sinks, "out_weight": out_weight, "residual_in": residual_in, "norm_gain": norm_gain, "expert_ids": expert_ids, "gate_weights": gate_weights, "gate_up": gate_up, "down_weight": down_weight}


def reference(queries, keys_values, sinks, out_weight, residual_in, norm_gain, expert_ids, gate_weights, gate_up, down_weight):
    group_size = HEADS // KV_HEADS
    block_count = TOKENS // WIN
    padded = jnp.concatenate([jnp.zeros((WIN, KV_HEADS, 2 * HD), jnp.bfloat16), keys_values], 0)
    window_kv = jnp.concatenate([padded[:-WIN].reshape(block_count, WIN, KV_HEADS, 2 * HD), padded[WIN:].reshape(block_count, WIN, KV_HEADS, 2 * HD)], 1)
    query_pos = jnp.arange(block_count)[:, None] * WIN + jnp.arange(WIN)[None, :]
    key_pos = jnp.arange(block_count)[:, None] * WIN - WIN + jnp.arange(2 * WIN)[None, :]
    distance = query_pos[:, :, None] - key_pos[:, None, :]
    allowed = (distance >= 0) & (distance < WIN) & (key_pos[:, None, :] >= 0)

    def per_head(operands):
        query_part, kv_part, sink_part = operands
        scores = jnp.einsum('nqgd,nkd->ngqk', query_part.astype(jnp.float32), kv_part[..., :HD].astype(jnp.float32)) * HD ** (-0.5)
        masked = jnp.where(allowed[:, None], scores, -1e+30)
        highest = jnp.maximum(masked.max(-1), sink_part[None, :, None])
        weights = jnp.where(allowed[:, None], jnp.exp(scores - highest[..., None]), 0.0)
        totals = weights.sum(-1) + jnp.exp(sink_part[None, :, None] - highest)
        rounded = weights.astype(jnp.bfloat16)
        weighed = jnp.einsum('ngqk,nkd->nqgd', rounded.astype(jnp.float32), kv_part[..., HD:].astype(jnp.float32))
        return (weighed / jnp.transpose(totals, (0, 2, 1))[..., None]).astype(jnp.bfloat16)
    query_blocks = queries.reshape(block_count, WIN, KV_HEADS, group_size, HD).transpose(2, 0, 1, 3, 4)
    heads_out = lax.map(per_head, (query_blocks, window_kv.transpose(2, 0, 1, 3), sinks.reshape(KV_HEADS, group_size)))
    attention = heads_out.transpose(1, 2, 0, 3, 4).reshape(TOKENS, HEADS * HD)
    hidden_state = residual_in.astype(jnp.float32) + jnp.dot(attention, out_weight, preferred_element_type=jnp.float32)
    normed = (hidden_state * lax.rsqrt(lax.optimization_barrier(jnp.mean(hidden_state * hidden_state, -1, keepdims=True)) + 1e-05) * norm_gain).astype(jnp.bfloat16)
    pair_ids = expert_ids.reshape(N_CTX, TOK_DEV * TOP)
    one_hot = (pair_ids[..., None] == jnp.arange(EXPERTS)[None, None, :]).astype(jnp.int32)
    slot_rank = lax.optimization_barrier(jnp.sum((jnp.cumsum(one_hot, 1) - one_hot) * one_hot, -1))
    row_index = (jnp.arange(N_CTX)[:, None] * CAP + slot_rank).reshape(-1).astype(jnp.int32)
    token_index = jnp.repeat(jnp.arange(TOKENS), TOP).astype(jnp.int32)
    flat_ids = pair_ids.reshape(-1).astype(jnp.int32)
    buffers = jnp.zeros((EXPERTS, N_CTX * CAP, D), jnp.bfloat16).at[flat_ids, row_index].set(normed[token_index])
    share = FF // SPLITS

    def per_expert(operands):
        expert_rows, weights_in, weights_out = operands
        gate_part = jnp.dot(expert_rows, weights_in[:, 0, :], preferred_element_type=jnp.float32)
        up_part = jnp.dot(expert_rows, weights_in[:, 1, :], preferred_element_type=jnp.float32)
        activated = ((up_part + 1.0) * gate_part * jax.nn.sigmoid(1.702 * gate_part)).astype(jnp.bfloat16)
        partial_value = jnp.einsum('rsf,dsf->srd', activated.reshape(-1, SPLITS, share).astype(jnp.float32), weights_out.reshape(D, SPLITS, share).astype(jnp.float32))
        rounded = lax.optimization_barrier(partial_value.astype(jnp.bfloat16))
        return lax.optimization_barrier(jnp.sum(rounded.astype(jnp.float32), 0))
    expert_out = lax.map(per_expert, (buffers, gate_up, down_weight))
    picked = expert_out[flat_ids, row_index].reshape(TOKENS, TOP, D)
    mixture = lax.optimization_barrier(jnp.sum(gate_weights[..., None] * picked, 1))
    return (hidden_state + mixture).astype(jnp.bfloat16)
```

```python
import functools

import jax
import jax.numpy as jnp
from jax import lax
from jax.experimental import pallas as pl
from jax.experimental.pallas import tpu as pltpu
from jax.sharding import PartitionSpec as P

D = 2880
HEADS = 64
KV_HEADS = 8
HD = 64
WIN = 128
EXPERTS = 16
TOP = 4
CAP = 40


def from_behind(value, axis, steps):
    count = lax.axis_size(axis)
    leading, last = (max(0, -steps), min(count, count - steps))
    return lax.ppermute(value, axis, [(source, source + steps) for source in range(leading, last)])


def shards(
    queries,
    keys_values,
    sinks,
    out_weight,
    residual_in,
    norm_gain,
    expert_ids,
    gate_weights,
    gate_up,
    down_weight,
):
    tok_rows = queries.shape[0]
    local_heads = sinks.shape[0]
    group_size = HEADS // KV_HEADS
    edge_rows = from_behind(keys_values, "ctx", 1)
    window_kv = jnp.concatenate([edge_rows, keys_values], 0)
    shared_head = (lax.axis_index("sub") * local_heads + jnp.arange(local_heads)) // group_size
    key_heads = jnp.take(window_kv[..., :HD], shared_head, axis=1)
    value_heads = jnp.take(window_kv[..., HD:], shared_head, axis=1)
    query_heads = queries.reshape(tok_rows, local_heads, HD)
    scores = jnp.einsum(
        "qhd,khd->hqk", query_heads, key_heads, preferred_element_type=jnp.float32
    ) * HD ** (-0.5)
    offset = lax.axis_index("ctx") * tok_rows
    query_pos = offset + jnp.arange(tok_rows)
    key_pos = offset - WIN + jnp.arange(WIN + tok_rows)
    distance = query_pos[:, None] - key_pos[None, :]
    allowed = (distance >= 0) & (distance < WIN) & (key_pos[None, :] >= 0)
    masked = jnp.where(allowed[None], scores, -1e30)
    highest = jnp.maximum(masked.max(-1), sinks[:, None])
    weights = jnp.where(allowed[None], jnp.exp(scores - highest[..., None]), 0.0)
    totals = weights.sum(-1) + jnp.exp(sinks[:, None] - highest)
    weighed = jnp.einsum(
        "hqk,khd->qhd",
        weights.astype(jnp.bfloat16),
        value_heads,
        preferred_element_type=jnp.float32,
    )
    attended = (
        (weighed / totals.T[..., None]).astype(jnp.bfloat16).reshape(tok_rows, local_heads * HD)
    )
    width_share = residual_in.shape[1]
    column_start = lax.axis_index(("head", "sub")) * width_share
    projected_attn = jnp.dot(attended, out_weight, preferred_element_type=jnp.float32)
    own_columns = lax.dynamic_slice_in_dim(
        projected_attn, column_start, width_share, 1
    ) + residual_in.astype(jnp.float32)
    projected_attn = lax.dynamic_update_slice_in_dim(projected_attn, own_columns, column_start, 1)
    hidden_state = lax.psum(projected_attn.astype(jnp.bfloat16), ("head", "sub")).astype(
        jnp.float32
    )
    normed = (
        hidden_state
        * lax.rsqrt(jnp.mean(hidden_state * hidden_state, -1, keepdims=True) + 1e-05)
        * norm_gain
    ).astype(jnp.bfloat16)
    flat_ids = expert_ids.reshape(-1)
    one_hot = (flat_ids[:, None] == jnp.arange(EXPERTS)[None, :]).astype(jnp.int32)
    slot_rank = jnp.sum((jnp.cumsum(one_hot, 0) - one_hot) * one_hot, -1)
    slot_index = flat_ids * CAP + slot_rank
    slot_match = jnp.arange(EXPERTS * CAP)[:, None] == slot_index[None, :]
    picker = jnp.any(slot_match.reshape(EXPERTS * CAP, tok_rows, TOP), -1).astype(jnp.bfloat16)
    outgoing = jnp.dot(picker, normed, preferred_element_type=jnp.bfloat16).reshape(
        EXPERTS, 1, CAP, D
    )
    arrived = lax.all_to_all(outgoing, "ctx", split_axis=0, concat_axis=1, tiled=True)
    local_experts = gate_up.shape[0]
    share = gate_up.shape[3]
    expert_rows = arrived.reshape(local_experts, -1, D)
    projected = jnp.einsum(
        "erd,edf->erf",
        expert_rows,
        gate_up.reshape(local_experts, D, 2 * share),
        preferred_element_type=jnp.float32,
    )
    gate_part = projected[..., :share]
    up_part = projected[..., share:]
    activated = ((up_part + 1.0) * gate_part * jax.nn.sigmoid(1.702 * gate_part)).astype(
        jnp.bfloat16
    )
    resid_cols = lax.dynamic_slice_in_dim(hidden_state, column_start, width_share, 1)
    summed = lax.psum_scatter(
        jnp.einsum(
            "ecf,erf->cer", down_weight, activated, preferred_element_type=jnp.float32
        ).astype(jnp.bfloat16),
        ("head", "sub"),
        scatter_dimension=0,
        tiled=True,
    ).astype(jnp.float32)
    regrouped = summed.reshape(width_share, local_experts, -1, CAP)
    returned = lax.all_to_all(
        regrouped.astype(jnp.bfloat16), "ctx", split_axis=2, concat_axis=1, tiled=True
    ).astype(regrouped.dtype)
    combiner = jnp.sum(
        jnp.where(slot_match, gate_weights.reshape(-1)[None, :], 0.0).reshape(
            EXPERTS * CAP, tok_rows, TOP
        ),
        -1,
    )
    mixture = jnp.dot(
        returned.reshape(width_share, EXPERTS * CAP),
        combiner,
        precision=lax.Precision.HIGHEST,
        preferred_element_type=jnp.float32,
    ).T
    return (resid_cols + mixture).astype(jnp.bfloat16)


BF = jnp.bfloat16
F32 = jnp.float32
MESH = pl.DeviceIdType.MESH
ROWS = 48
EXTRA = 16
NT = (((1,), (1,)), ((), ()))
TN = (((0,), (0,)), ((), ()))


def fused_kernel(
    q_ref,
    kv_ref,
    sinks_ref,
    ow_hbm,
    resid_ref,
    gain_ref,
    info_ref,
    gu_hbm,
    dn_hbm,
    out_ref,
    kvprev,
    ow,
    gu,
    dn,
    att,
    pa,
    ra,
    hidden,
    info,
    xb,
    xsel,
    actt,
    outs,
    ptc,
    mix,
    rsib,
    xq,
    rx,
    zq,
    rz,
    w_sem,
    kv_sem,
    info_send,
    info_recv,
    a_send,
    a_recv,
    b_send,
    b_recv,
    c_send,
    csib_recv,
    cx_recv,
    cz_recv,
):
    g, c, h, s = (lax.axis_index(n) for n in ("groups", "ctx", "head", "sub"))
    n_ctx = 4
    toks = q_ref.shape[0]
    share = resid_ref.shape[0]
    experts = gu_hbm.shape[0]
    gu_slots, dn_slots = gu.shape[0], dn.shape[0]
    quarter = lambda hh, ss: hh * 2 + ss
    me_j, x_j = quarter(h, s), quarter(1 - h, s)
    sib, xdev = (g, c, h, 1 - s), (g, c, 1 - h, s)
    zdev = lambda cc: (g, cc, h, s)
    rows_of = lambda j: pl.ds(pl.multiple_of(j * share, 16), share)

    def remote(src, dst, send, recv, dev):
        return pltpu.make_async_remote_copy(
            src_ref=src, dst_ref=dst, send_sem=send, recv_sem=recv, device_id=dev, device_id_type=MESH
        )

    ow_copy = pltpu.make_async_copy(ow_hbm, ow, w_sem.at[0])
    gu_copy = lambda e, slot: pltpu.make_async_copy(gu_hbm.at[e], gu.at[slot], w_sem.at[1 + slot])
    dn_copy = lambda e, slot: pltpu.make_async_copy(
        dn_hbm.at[e], dn.at[slot], w_sem.at[1 + gu_slots + slot]
    )
    ow_copy.start()
    for e in range(gu_slots):
        gu_copy(e, e).start()
        if e < dn_slots:
            dn_copy(e, e).start()

    barrier = pltpu.get_barrier_semaphore()
    others = [lax.rem(c + i, n_ctx) for i in range(1, n_ctx)]
    for dev in [sib, xdev] + [zdev(o) for o in others]:
        pl.semaphore_signal(barrier, inc=1, device_id=dev, device_id_type=MESH)
    pl.semaphore_wait(barrier, 2 + len(others))

    kv_out = remote(kv_ref, kvprev, kv_sem.at[0], kv_sem.at[1], zdev(lax.rem(c + 1, n_ctx)))

    @pl.when(c < n_ctx - 1)
    def _():
        kv_out.start()

    info[c] = info_ref[...]
    for i, o in enumerate(others):
        remote(info_ref, info.at[c], info_send.at[i], info_recv.at[c], zdev(o)).start()

    @pl.when(c > 0)
    def _():
        kv_out.wait_recv()

    @pl.when(c == 0)
    def _():
        kvprev[...] = jnp.zeros_like(kvprev)

    t_pos = lax.broadcasted_iota(jnp.int32, (toks, 2 * toks), 0)
    k_pos = lax.broadcasted_iota(jnp.int32, (toks, 2 * toks), 1)
    first = jnp.where(c == 0, toks, 0)
    allowed = (k_pos <= t_pos + WIN) & (k_pos > t_pos) & (k_pos >= first)
    group = HEADS // KV_HEADS

    def head_pair(p, carry):
        kv_cols = pl.ds(pl.multiple_of((2 * p // group) * 2 * HD, 2 * HD), 2 * HD)
        q_cols = pl.ds(pl.multiple_of(p * 2 * HD, 2 * HD), 2 * HD)
        window = jnp.concatenate([kvprev[:, kv_cols], kv_ref[:, kv_cols]], 0)
        keys, values = window[:, :HD], window[:, HD:]
        pair = q_ref[:, q_cols]
        done = []
        for i in range(2):
            sink = sinks_ref[2 * p + i]
            scores = lax.dot_general(
                pair[:, i * HD : (i + 1) * HD], keys, NT, preferred_element_type=F32
            ) * HD ** (-0.5)
            masked = jnp.where(allowed, scores, -1e30)
            highest = jnp.maximum(jnp.max(masked, -1, keepdims=True), sink)
            weights = jnp.where(allowed, jnp.exp(masked - highest), 0.0)
            totals = jnp.sum(weights, -1, keepdims=True) + jnp.exp(sink - highest)
            weighed = jnp.dot(weights.astype(BF), values, preferred_element_type=F32)
            done.append(weighed / totals)
        att[:, q_cols] = jnp.concatenate(done, 1).astype(BF)
        return carry

    lax.fori_loop(0, q_ref.shape[1] // (2 * HD), head_pair, 0)

    ow_copy.wait()

    def projected(j):
        return lax.dot_general(ow[rows_of(j), :], att[...], NT, preferred_element_type=F32)

    for i, hh in enumerate((1 - h, h)):
        pa[i] = projected(quarter(hh, 1 - s)).astype(BF)
        remote(pa.at[i], ra.at[i], a_send.at[i], a_recv.at[i], sib).start()
    across = projected(x_j)
    remote(pa.at[0], ra.at[0], a_send.at[0], a_recv.at[0], sib).wait_recv()
    pa[2] = (across + ra[0].astype(F32)).astype(BF)
    to_x = remote(pa.at[2], ra.at[2], a_send.at[2], a_recv.at[2], xdev)
    to_x.start()
    own = projected(me_j) + resid_ref[...].astype(F32)
    remote(pa.at[1], ra.at[1], a_send.at[1], a_recv.at[1], sib).wait_recv()
    own = own + ra[1].astype(F32)
    to_x.wait_recv()
    own = own + ra[2].astype(F32)
    hidden[...] = own

    xb[me_j * n_ctx + c, :share, :] = (own * gain_ref[...]).astype(BF)
    squares = jnp.sum(own * own, 0, keepdims=True)
    upper = squares.astype(BF).astype(F32)
    line = lax.broadcasted_iota(jnp.int32, (EXTRA, toks), 0)
    xb[me_j * n_ctx + c, share:, :] = jnp.where(
        line == 0, upper, jnp.where(line == 1, squares - upper, 0.0)
    ).astype(BF)

    def block(j, cc, send, dev):
        k = j * n_ctx + cc
        return remote(xb.at[k], xb.at[k], b_send.at[send], b_recv.at[k], dev)

    order = [c] + others
    for i, o in enumerate(others):
        block(me_j, c, i, zdev(o)).start()
    for i, o in enumerate(order):
        if i > 0:
            block(me_j, o, 0, sib).wait_recv()
        block(me_j, o, 3 + i, xdev).start()
        block(me_j, o, 7 + i, sib).start()
    for i, o in enumerate(order):
        block(x_j, o, 0, sib).wait_recv()
        block(x_j, o, 11 + i, sib).start()
    for o in others:
        remote(info_ref, info.at[o], info_send.at[0], info_recv.at[o], sib).wait_recv()
    for o in order:
        for hh in (h, 1 - h):
            block(quarter(hh, 1 - s), o, 0, sib).wait_recv()

    total_sq = jnp.zeros((n_ctx, toks), F32)
    for j in range(4):
        tails = [
            jnp.sum(xb[j * n_ctx + cc, share:, :].astype(F32), 0, keepdims=True)
            for cc in range(n_ctx)
        ]
        total_sq = total_sq + jnp.concatenate(tails, 0)
    scale = lax.rsqrt(total_sq / D + 1e-05)
    scale = jnp.concatenate([scale[cc : cc + 1] for cc in range(n_ctx)], 1)
    s_hi = scale.astype(BF).astype(F32)
    s_mid = (scale - s_hi).astype(BF).astype(F32)
    s_lo = scale - s_hi - s_mid
    tri = (
        lax.broadcasted_iota(jnp.int32, (toks, toks), 0)
        < lax.broadcasted_iota(jnp.int32, (toks, toks), 1)
    )
    tri = jnp.where(tri, 1.0, 0.0).astype(BF)
    line8 = lax.broadcasted_iota(jnp.int32, (16, n_ctx * toks), 0)
    scales = jnp.where(
        line8 == 0, s_hi, jnp.where(line8 == 1, s_mid, jnp.where(line8 == 2, s_lo, 0.0))
    ).astype(BF)
    all_rows = lax.broadcasted_iota(jnp.int32, (n_ctx * ROWS, toks), 0).astype(F32)
    slot_rows = lax.broadcasted_iota(jnp.int32, (ROWS, toks), 0).astype(F32)
    tile = 240 if share % 240 == 0 else share
    width = 768

    def expert(e, carry):
        name = (c * experts + e).astype(F32)
        places, factors = [], []
        for cc in range(n_ctx):
            routing = info[cc]
            same = jnp.where(routing[:TOP] == name, 1.0, 0.0)
            named = jnp.sum(same, 0, keepdims=True)
            factor = jnp.sum(same * routing[TOP:], 0, keepdims=True)
            rank = jnp.dot(
                jnp.broadcast_to(named, (16, toks)).astype(BF), tri, preferred_element_type=F32
            )[:1]
            place = jnp.where(named > 0, rank, -1.0)
            ptc[cc, pl.ds(pl.multiple_of(e * ROWS, 16), ROWS), :] = jnp.where(
                slot_rows == place, 1.0, 0.0
            ).astype(BF)
            places.append(jnp.where(all_rows == jnp.where(named > 0, rank + cc * ROWS, -1.0), 1.0, 0.0))
            factors.append(jnp.sum(places[-1] * factor, 1, keepdims=True))
        pick = jnp.concatenate(places, 1).astype(BF)
        factor = factors[0] + factors[1] + factors[2] + factors[3]
        row_scale = jnp.sum(
            lax.dot_general(scales, pick, NT, preferred_element_type=F32), 0, keepdims=True
        )

        def select(j, carry):
            features = jnp.concatenate([xb[j * n_ctx + cc, :share, :] for cc in range(n_ctx)], 1)
            xsel[rows_of(j), :] = lax.dot_general(
                features, pick, NT, preferred_element_type=F32
            ).astype(BF)
            return carry

        lax.fori_loop(0, 4, select, 0)
        slot = lax.rem(e, gu_slots)
        gu_copy(e, slot).wait()

        def up_gate(i, carry):
            rows = pl.ds(pl.multiple_of(i * tile, 16), tile)
            gate = jnp.dot(gu[slot, 0, rows, :], xsel[...], preferred_element_type=F32) * row_scale
            up = jnp.dot(gu[slot, 1, rows, :], xsel[...], preferred_element_type=F32) * row_scale
            actt[rows, :] = ((up + 1.0) * gate * jax.nn.sigmoid(1.702 * gate)).astype(BF)
            return carry

        lax.fori_loop(0, share // tile, up_gate, 0)

        @pl.when(e + gu_slots < experts)
        def _():
            gu_copy(e + gu_slots, slot).start()

        dslot = lax.rem(e, dn_slots)
        dn_copy(e, dslot).wait()
        act = actt[...]
        for lo in range(0, D, width):
            hi = min(D, lo + width)
            res = lax.dot_general(act, dn[dslot, :, lo:hi], TN, preferred_element_type=F32)
            res = (res * factor).astype(BF)
            for cc in range(n_ctx):
                outs[cc, pl.ds(pl.multiple_of(e * ROWS, 16), ROWS), lo:hi] = res[
                    cc * ROWS : (cc + 1) * ROWS
                ]

        @pl.when(e + dn_slots < experts)
        def _():
            dn_copy(e + dn_slots, dslot).start()

        return carry

    lax.fori_loop(0, experts, expert, 0)

    back = others + [c]
    for i, o in enumerate(back):
        for lo in range(0, D, width):
            hi = min(D, lo + width)
            mix[o, lo:hi, :] = lax.dot_general(
                outs[o, :, lo:hi], ptc[o], TN, preferred_element_type=F32
            ).astype(BF)
        for hh in range(2):
            remote(
                mix.at[o, rows_of(quarter(hh, 1 - s))],
                rsib.at[o * 2 + hh],
                c_send.at[i * 2 + hh],
                csib_recv.at[o * 2 + hh],
                sib,
            ).start()

    def wait_sib(o, hh):
        k = o * 2 + hh
        remote(rsib.at[k], rsib.at[k], c_send.at[0], csib_recv.at[k], sib).wait_recv()
        return rsib[k].astype(F32)

    for i, o in enumerate(back):
        xq[o] = (mix[o, rows_of(x_j), :].astype(F32) + wait_sib(o, 1 - h)).astype(BF)
        remote(xq.at[o], rx.at[o], c_send.at[8 + i], cx_recv.at[o], xdev).start()
    for i, o in enumerate(back):
        part = mix[o, rows_of(me_j), :].astype(F32) + wait_sib(o, h)
        remote(xq.at[o], rx.at[o], c_send.at[0], cx_recv.at[o], xdev).wait_recv()
        part = part + rx[o].astype(F32)
        if i < n_ctx - 1:
            zq[i] = part.astype(BF)
            remote(zq.at[i], rz.at[c], c_send.at[12 + i], cz_recv.at[c], zdev(o)).start()
        else:
            hidden[...] = hidden[...] + part
    for o in others:
        remote(zq.at[0], rz.at[o], c_send.at[0], cz_recv.at[o], sib).wait_recv()
        hidden[...] = hidden[...] + rz[o].astype(F32)
    out_ref[...] = hidden[...].astype(BF)

    @pl.when(c < n_ctx - 1)
    def _():
        kv_out.wait_send()

    for i in range(n_ctx - 1):
        remote(info_ref, info.at[c], info_send.at[i], info_recv.at[c], sib).wait_send()
    for i in range(3):
        remote(pa.at[i], ra.at[i], a_send.at[i], a_recv.at[i], sib).wait_send()
    for i in range(15):
        block(me_j, c, i, sib).wait_send()
    for i in range(15):
        remote(rx.at[0], rx.at[0], c_send.at[i], cx_recv.at[0], sib).wait_send()


def fused_shards(
    queries,
    keys_values,
    sinks,
    out_weight,
    residual_in,
    norm_gain,
    expert_ids,
    gate_weights,
    gate_up,
    down_weight,
):
    toks = queries.shape[0]
    share = residual_in.shape[1]
    experts = gate_up.shape[0]
    kv_heads = sinks.shape[0] * KV_HEADS // HEADS
    kv = lax.dynamic_slice_in_dim(keys_values, lax.axis_index("sub") * kv_heads, kv_heads, 1)
    kv = kv.reshape(toks, kv_heads * 2 * HD)
    gain = lax.dynamic_slice_in_dim(norm_gain, lax.axis_index(("head", "sub")) * share, share, 0)
    info = jnp.concatenate([expert_ids.T.astype(F32), gate_weights.T], 0)
    vmem = pl.BlockSpec(memory_space=pltpu.VMEM)
    hbm = pl.BlockSpec(memory_space=pl.ANY)
    gu_slots, dn_slots = min(3, experts), min(2, experts)
    dma = pltpu.SemaphoreType.DMA
    out = pl.pallas_call(
        fused_kernel,
        out_shape=jax.ShapeDtypeStruct((share, toks), BF),
        in_specs=[vmem, vmem, pl.BlockSpec(memory_space=pltpu.SMEM), hbm, vmem, vmem, vmem, hbm, hbm],
        out_specs=vmem,
        scratch_shapes=[
            pltpu.VMEM(kv.shape, BF),
            pltpu.VMEM((D, out_weight.shape[0]), BF),
            pltpu.VMEM((gu_slots, 2, share, D), BF),
            pltpu.VMEM((dn_slots, share, D), BF),
            pltpu.VMEM(queries.shape, BF),
            pltpu.VMEM((3, share, toks), BF),
            pltpu.VMEM((3, share, toks), BF),
            pltpu.VMEM((share, toks), F32),
            pltpu.VMEM((4, 2 * TOP, toks), F32),
            pltpu.VMEM((16, share + EXTRA, toks), BF),
            pltpu.VMEM((D, 4 * ROWS), BF),
            pltpu.VMEM((share, 4 * ROWS), BF),
            pltpu.VMEM((4, experts * ROWS, D), BF),
            pltpu.VMEM((4, experts * ROWS, toks), BF),
            pltpu.VMEM((4, D, toks), BF),
            pltpu.VMEM((8, share, toks), BF),
            pltpu.VMEM((4, share, toks), BF),
            pltpu.VMEM((4, share, toks), BF),
            pltpu.VMEM((3, share, toks), BF),
            pltpu.VMEM((4, share, toks), BF),
            dma((1 + gu_slots + dn_slots,)),
            dma((2,)),
            dma((3,)),
            dma((4,)),
            dma((3,)),
            dma((3,)),
            dma((15,)),
            dma((16,)),
            dma((15,)),
            dma((8,)),
            dma((4,)),
            dma((4,)),
        ],
        compiler_params=pltpu.CompilerParams(
            collective_id=0, has_side_effects=True, vmem_limit_bytes=63 * 1024 * 1024
        ),
    )(
        queries,
        kv,
        sinks,
        out_weight.T,
        residual_in.T,
        gain[:, None],
        info,
        gate_up.transpose(0, 2, 3, 1),
        down_weight.transpose(0, 2, 1),
    )
    return out.T


def solution(mesh):
    fits = mesh.shape["ctx"] == 4 and mesh.shape["head"] == 2 and mesh.shape["sub"] == 2
    return jax.shard_map(
        fused_shards if fits else shards,
        mesh=mesh,
        in_specs=(
            P(("groups", "ctx"), ("head", "sub")),
            P(("groups", "ctx"), "head", None),
            P(("head", "sub")),
            P(("head", "sub"), None),
            P(("groups", "ctx"), ("head", "sub")),
            P(),
            P(("groups", "ctx"), None),
            P(("groups", "ctx"), None),
            P("ctx", None, None, ("head", "sub")),
            P("ctx", None, ("head", "sub")),
        ),
        out_specs=P(("groups", "ctx"), ("head", "sub")),
        check_vma=False,
    )
```

```python
import functools

import jax
import jax.numpy as jnp
from jax import lax
from jax.experimental import pallas as pl
from jax.experimental.pallas import tpu as pltpu
from jax.sharding import PartitionSpec as P

D = 2880
HEADS = 64
KV_HEADS = 8
HD = 64
WIN = 128
EXPERTS = 16
TOP = 4
CAP = 40


def from_behind(value, axis, steps):
    count = lax.axis_size(axis)
    leading, last = (max(0, -steps), min(count, count - steps))
    return lax.ppermute(value, axis, [(source, source + steps) for source in range(leading, last)])


def shards(
    queries,
    keys_values,
    sinks,
    out_weight,
    residual_in,
    norm_gain,
    expert_ids,
    gate_weights,
    gate_up,
    down_weight,
):
    tok_rows = queries.shape[0]
    local_heads = sinks.shape[0]
    group_size = HEADS // KV_HEADS
    edge_rows = from_behind(keys_values, "ctx", 1)
    window_kv = jnp.concatenate([edge_rows, keys_values], 0)
    shared_head = (lax.axis_index("sub") * local_heads + jnp.arange(local_heads)) // group_size
    key_heads = jnp.take(window_kv[..., :HD], shared_head, axis=1)
    value_heads = jnp.take(window_kv[..., HD:], shared_head, axis=1)
    query_heads = queries.reshape(tok_rows, local_heads, HD)
    scores = jnp.einsum(
        "qhd,khd->hqk", query_heads, key_heads, preferred_element_type=jnp.float32
    ) * HD ** (-0.5)
    offset = lax.axis_index("ctx") * tok_rows
    query_pos = offset + jnp.arange(tok_rows)
    key_pos = offset - WIN + jnp.arange(WIN + tok_rows)
    distance = query_pos[:, None] - key_pos[None, :]
    allowed = (distance >= 0) & (distance < WIN) & (key_pos[None, :] >= 0)
    masked = jnp.where(allowed[None], scores, -1e30)
    highest = jnp.maximum(masked.max(-1), sinks[:, None])
    weights = jnp.where(allowed[None], jnp.exp(scores - highest[..., None]), 0.0)
    totals = weights.sum(-1) + jnp.exp(sinks[:, None] - highest)
    weighed = jnp.einsum(
        "hqk,khd->qhd",
        weights.astype(jnp.bfloat16),
        value_heads,
        preferred_element_type=jnp.float32,
    )
    attended = (
        (weighed / totals.T[..., None]).astype(jnp.bfloat16).reshape(tok_rows, local_heads * HD)
    )
    width_share = residual_in.shape[1]
    column_start = lax.axis_index(("head", "sub")) * width_share
    projected_attn = jnp.dot(attended, out_weight, preferred_element_type=jnp.float32)
    own_columns = lax.dynamic_slice_in_dim(
        projected_attn, column_start, width_share, 1
    ) + residual_in.astype(jnp.float32)
    projected_attn = lax.dynamic_update_slice_in_dim(projected_attn, own_columns, column_start, 1)
    hidden_state = lax.psum(projected_attn.astype(jnp.bfloat16), ("head", "sub")).astype(
        jnp.float32
    )
    normed = (
        hidden_state
        * lax.rsqrt(jnp.mean(hidden_state * hidden_state, -1, keepdims=True) + 1e-05)
        * norm_gain
    ).astype(jnp.bfloat16)
    flat_ids = expert_ids.reshape(-1)
    one_hot = (flat_ids[:, None] == jnp.arange(EXPERTS)[None, :]).astype(jnp.int32)
    slot_rank = jnp.sum((jnp.cumsum(one_hot, 0) - one_hot) * one_hot, -1)
    slot_index = flat_ids * CAP + slot_rank
    slot_match = jnp.arange(EXPERTS * CAP)[:, None] == slot_index[None, :]
    picker = jnp.any(slot_match.reshape(EXPERTS * CAP, tok_rows, TOP), -1).astype(jnp.bfloat16)
    outgoing = jnp.dot(picker, normed, preferred_element_type=jnp.bfloat16).reshape(
        EXPERTS, 1, CAP, D
    )
    arrived = lax.all_to_all(outgoing, "ctx", split_axis=0, concat_axis=1, tiled=True)
    local_experts = gate_up.shape[0]
    share = gate_up.shape[3]
    expert_rows = arrived.reshape(local_experts, -1, D)
    projected = jnp.einsum(
        "erd,edf->erf",
        expert_rows,
        gate_up.reshape(local_experts, D, 2 * share),
        preferred_element_type=jnp.float32,
    )
    gate_part = projected[..., :share]
    up_part = projected[..., share:]
    activated = ((up_part + 1.0) * gate_part * jax.nn.sigmoid(1.702 * gate_part)).astype(
        jnp.bfloat16
    )
    resid_cols = lax.dynamic_slice_in_dim(hidden_state, column_start, width_share, 1)
    summed = lax.psum_scatter(
        jnp.einsum(
            "ecf,erf->cer", down_weight, activated, preferred_element_type=jnp.float32
        ).astype(jnp.bfloat16),
        ("head", "sub"),
        scatter_dimension=0,
        tiled=True,
    ).astype(jnp.float32)
    regrouped = summed.reshape(width_share, local_experts, -1, CAP)
    returned = lax.all_to_all(
        regrouped.astype(jnp.bfloat16), "ctx", split_axis=2, concat_axis=1, tiled=True
    ).astype(regrouped.dtype)
    combiner = jnp.sum(
        jnp.where(slot_match, gate_weights.reshape(-1)[None, :], 0.0).reshape(
            EXPERTS * CAP, tok_rows, TOP
        ),
        -1,
    )
    mixture = jnp.dot(
        returned.reshape(width_share, EXPERTS * CAP),
        combiner,
        precision=lax.Precision.HIGHEST,
        preferred_element_type=jnp.float32,
    ).T
    return (resid_cols + mixture).astype(jnp.bfloat16)


BF = jnp.bfloat16
F32 = jnp.float32
MESH = pl.DeviceIdType.MESH
ROWS = 48
EXTRA = 16
NT = (((1,), (1,)), ((), ()))
TN = (((0,), (0,)), ((), ()))


def fused_kernel(
    q_ref,
    kv_ref,
    sinks_ref,
    ow_hbm,
    resid_ref,
    gain_ref,
    ids_ref,
    gates_ref,
    gu_hbm,
    dn_hbm,
    out_ref,
    kvown,
    picks,
    factors_of,
    kvprev,
    ow,
    gu,
    dn,
    att,
    pa,
    ra,
    hidden,
    info,
    xb,
    xsel,
    actt,
    outs,
    ptc,
    mix,
    rsib,
    rx,
    rz,
    w_sem,
    kv_sem,
    info_send,
    info_recv,
    a_send,
    a_recv,
    b_send,
    b_recv,
    c_send,
    csib_recv,
    cx_recv,
    cz_recv,
):
    g, c, h, s = (lax.axis_index(n) for n in ("groups", "ctx", "head", "sub"))
    n_ctx = 4
    toks = q_ref.shape[0]
    share = resid_ref.shape[0]
    experts = gu_hbm.shape[0]
    gu_slots, dn_slots = gu.shape[0], dn.shape[0]
    quarter = lambda hh, ss: hh * 2 + ss
    me_j, x_j = quarter(h, s), quarter(1 - h, s)
    sib, xdev = (g, c, h, 1 - s), (g, c, 1 - h, s)
    zdev = lambda cc: (g, cc, h, s)
    rows_of = lambda j: pl.ds(pl.multiple_of(j * share, 16), share)

    def remote(src, dst, send, recv, dev):
        return pltpu.make_async_remote_copy(
            src_ref=src, dst_ref=dst, send_sem=send, recv_sem=recv, device_id=dev, device_id_type=MESH
        )

    ow_copy = pltpu.make_async_copy(ow_hbm, ow, w_sem.at[0])
    gu_copy = lambda e, slot: pltpu.make_async_copy(gu_hbm.at[e], gu.at[slot], w_sem.at[1 + slot])
    dn_copy = lambda e, slot: pltpu.make_async_copy(
        dn_hbm.at[e], dn.at[slot], w_sem.at[1 + gu_slots + slot]
    )
    ow_copy.start()
    for e in range(gu_slots):
        gu_copy(e, e).start()
        if e < dn_slots:
            dn_copy(e, e).start()

    heads = kvown.shape[1] // (2 * HD)
    for p in range(heads):
        kvown[:, p * 2 * HD : (p + 1) * 2 * HD] = jnp.where(
            s == 0, kv_ref[:, p, :], kv_ref[:, p + kv_ref.shape[1] - heads, :]
        )
    info[c, :TOP, :] = ids_ref[...].astype(F32)
    info[c, TOP:, :] = gates_ref[...]

    barrier = pltpu.get_barrier_semaphore()
    others = [lax.rem(c + i, n_ctx) for i in range(1, n_ctx)]
    for dev in [sib, xdev] + [zdev(o) for o in others]:
        pl.semaphore_signal(barrier, inc=1, device_id=dev, device_id_type=MESH)
    pl.semaphore_wait(barrier, 2 + len(others))

    kv_out = remote(kvown, kvprev, kv_sem.at[0], kv_sem.at[1], zdev(lax.rem(c + 1, n_ctx)))

    @pl.when(c < n_ctx - 1)
    def _():
        kv_out.start()

    for i, o in enumerate(others):
        remote(info.at[c], info.at[c], info_send.at[i], info_recv.at[c], zdev(o)).start()

    line4 = lax.broadcasted_iota(jnp.int32, gain_ref.shape, 0)
    own_gain = jnp.sum(jnp.where(line4 == me_j, gain_ref[...], 0.0), 0, keepdims=True)
    hidden[...] = jnp.broadcast_to(own_gain, (toks, share)).T

    @pl.when(c > 0)
    def _():
        kv_out.wait_recv()

    @pl.when(c == 0)
    def _():
        kvprev[...] = jnp.zeros_like(kvprev)

    t_pos = lax.broadcasted_iota(jnp.int32, (toks, 2 * toks), 0)
    k_pos = lax.broadcasted_iota(jnp.int32, (toks, 2 * toks), 1)
    first = jnp.where(c == 0, toks, 0)
    allowed = (k_pos <= t_pos + WIN) & (k_pos > t_pos) & (k_pos >= first)
    group = HEADS // KV_HEADS

    def head_pair(p, carry):
        kv_cols = pl.ds(pl.multiple_of((2 * p // group) * 2 * HD, 2 * HD), 2 * HD)
        q_cols = pl.ds(pl.multiple_of(p * 2 * HD, 2 * HD), 2 * HD)
        window = jnp.concatenate([kvprev[:, kv_cols], kvown[:, kv_cols]], 0)
        keys, values = window[:, :HD], window[:, HD:]
        pair = q_ref[:, q_cols]
        done = []
        for i in range(2):
            sink = sinks_ref[2 * p + i]
            scores = lax.dot_general(
                pair[:, i * HD : (i + 1) * HD], keys, NT, preferred_element_type=F32
            ) * HD ** (-0.5)
            masked = jnp.where(allowed, scores, -1e30)
            highest = jnp.maximum(jnp.max(masked, -1, keepdims=True), sink)
            weights = jnp.where(allowed, jnp.exp(masked - highest), 0.0)
            totals = jnp.sum(weights, -1, keepdims=True) + jnp.exp(sink - highest)
            weighed = jnp.dot(weights.astype(BF), values, preferred_element_type=F32)
            done.append(weighed / totals)
        att[:, q_cols] = jnp.concatenate(done, 1).astype(BF)
        return carry

    lax.fori_loop(0, q_ref.shape[1] // (2 * HD), head_pair, 0, unroll=2)

    ow_copy.wait()

    def projected(j):
        return lax.dot_general(ow[rows_of(j), :], att[...], NT, preferred_element_type=F32)

    for i, hh in enumerate((1 - h, h)):
        pa[i] = projected(quarter(hh, 1 - s)).astype(BF)
        remote(pa.at[i], ra.at[i], a_send.at[i], a_recv.at[i], sib).start()
    across = projected(x_j)
    remote(pa.at[0], ra.at[0], a_send.at[0], a_recv.at[0], sib).wait_recv()
    pa[2] = (across + ra[0].astype(F32)).astype(BF)
    to_x = remote(pa.at[2], ra.at[2], a_send.at[2], a_recv.at[2], xdev)
    to_x.start()
    own = projected(me_j) + resid_ref[...].astype(F32)
    remote(pa.at[1], ra.at[1], a_send.at[1], a_recv.at[1], sib).wait_recv()
    own = own + ra[1].astype(F32)
    to_x.wait_recv()
    own = own + ra[2].astype(F32)

    xb[me_j * n_ctx + c, :share, :] = (own * hidden[...]).astype(BF)
    hidden[...] = own
    squares = jnp.sum(own * own, 0, keepdims=True)
    upper = squares.astype(BF).astype(F32)
    line = lax.broadcasted_iota(jnp.int32, (EXTRA, toks), 0)
    xb[me_j * n_ctx + c, share:, :] = jnp.where(
        line == 0, upper, jnp.where(line == 1, squares - upper, 0.0)
    ).astype(BF)

    def block(j, cc, send, dev):
        k = j * n_ctx + cc
        return remote(xb.at[k], xb.at[k], b_send.at[send], b_recv.at[k], dev)

    def both_ways(d, act):
        for sign in (1,) if d == 0 else (-1, 1):
            o = c + sign * d
            inside = None if d == 0 else (o >= 0) & (o < n_ctx)

            def at(o=o, sign=sign):
                act(o, sign)

            at() if inside is None else pl.when(inside)(at)

    def z_step(d):
        def act(o, sign):
            if d > 0:
                block(me_j, o, 0, sib).wait_recv()
            for way in (1, -1) if d == 0 else (-sign,):

                @pl.when((c + way >= 0) & (c + way < n_ctx))
                def _():
                    block(me_j, o, d if way > 0 else 3 + d, zdev(c + way)).start()

            block(me_j, o, 6 + o, xdev).start()
            block(me_j, o, 10 + o, sib).start()

        both_ways(d, act)

    def x_step(d):
        def act(o, sign):
            block(x_j, o, 0, sib).wait_recv()
            block(x_j, o, 14 + o, sib).start()

        both_ways(d, act)

    z_step(0)
    for o in others:
        remote(info.at[o], info.at[o], info_send.at[0], info_recv.at[o], sib).wait_recv()

    tri = (
        lax.broadcasted_iota(jnp.int32, (toks, toks), 0)
        < lax.broadcasted_iota(jnp.int32, (toks, toks), 1)
    )
    tri = jnp.where(tri, 1.0, 0.0).astype(BF)
    all_rows = lax.broadcasted_iota(jnp.int32, (n_ctx * ROWS, toks), 0).astype(F32)
    slot_rows = lax.broadcasted_iota(jnp.int32, (ROWS, toks), 0).astype(F32)

    def route(e, carry):
        name = (c * experts + e).astype(F32)
        places, factors = [], []
        for cc in range(n_ctx):
            routing = info[cc]
            same = jnp.where(routing[:TOP] == name, 1.0, 0.0)
            named = jnp.sum(same, 0, keepdims=True)
            factor = jnp.sum(same * routing[TOP:], 0, keepdims=True)
            rank = jnp.dot(
                jnp.broadcast_to(named, (16, toks)).astype(BF), tri, preferred_element_type=F32
            )[:1]
            place = jnp.where(named > 0, rank, -1.0)
            ptc[cc, pl.ds(pl.multiple_of(e * ROWS, 16), ROWS), :] = jnp.where(
                slot_rows == place, 1.0, 0.0
            ).astype(BF)
            places.append(jnp.where(all_rows == jnp.where(named > 0, rank + cc * ROWS, -1.0), 1.0, 0.0))
            factors.append(jnp.sum(places[-1] * factor, 1, keepdims=True))
        picks[e] = jnp.concatenate(places, 1).astype(BF)
        factors_of[e] = factors[0] + factors[1] + factors[2] + factors[3]
        return carry

    lax.fori_loop(0, experts, route, 0)
    z_step(1)
    x_step(0)
    z_step(2)
    x_step(1)
    z_step(3)
    x_step(2)

    def select(j):
        features = jnp.concatenate([xb[j * n_ctx + cc, :share, :] for cc in range(n_ctx)], 1)

        def one(e, carry):
            xsel[e, rows_of(j), :] = lax.dot_general(
                features, picks[e], NT, preferred_element_type=F32
            ).astype(BF)
            return carry

        lax.fori_loop(0, experts, one, 0)

    select(me_j)
    order = [c] + others
    for o in order:
        block(quarter(h, 1 - s), o, 0, sib).wait_recv()
    select(quarter(h, 1 - s))
    x_step(3)
    select(x_j)
    for o in order:
        block(quarter(1 - h, 1 - s), o, 0, sib).wait_recv()
    select(quarter(1 - h, 1 - s))

    total_sq = jnp.zeros((n_ctx, toks), F32)
    for j in range(4):
        tails = [
            jnp.sum(xb[j * n_ctx + cc, share:, :].astype(F32), 0, keepdims=True)
            for cc in range(n_ctx)
        ]
        total_sq = total_sq + jnp.concatenate(tails, 0)
    scale = lax.rsqrt(total_sq / D + 1e-05)
    scale = jnp.concatenate([scale[cc : cc + 1] for cc in range(n_ctx)], 1)
    s_hi = scale.astype(BF).astype(F32)
    s_mid = (scale - s_hi).astype(BF).astype(F32)
    s_lo = scale - s_hi - s_mid
    line8 = lax.broadcasted_iota(jnp.int32, (16, n_ctx * toks), 0)
    scales = jnp.where(
        line8 == 0, s_hi, jnp.where(line8 == 1, s_mid, jnp.where(line8 == 2, s_lo, 0.0))
    ).astype(BF)
    tile = 240 if share % 240 == 0 else share
    width = 768

    def expert(e, carry):
        factor = factors_of[e]
        row_scale = jnp.sum(
            lax.dot_general(scales, picks[e], NT, preferred_element_type=F32), 0, keepdims=True
        )

        slot = lax.rem(e, gu_slots)
        gu_copy(e, slot).wait()

        def up_gate(i, carry):
            rows = pl.ds(pl.multiple_of(i * tile, 16), tile)
            gate = jnp.dot(gu[slot, 0, rows, :], xsel[e], preferred_element_type=F32) * row_scale
            up = jnp.dot(gu[slot, 1, rows, :], xsel[e], preferred_element_type=F32) * row_scale
            actt[rows, :] = ((up + 1.0) * gate * jax.nn.sigmoid(1.702 * gate)).astype(BF)
            return carry

        lax.fori_loop(0, share // tile, up_gate, 0)

        @pl.when(e + gu_slots < experts)
        def _():
            gu_copy(e + gu_slots, slot).start()

        dslot = lax.rem(e, dn_slots)
        dn_copy(e, dslot).wait()
        act = actt[...]
        for lo in range(0, D, width):
            hi = min(D, lo + width)
            res = lax.dot_general(act, dn[dslot, :, lo:hi], TN, preferred_element_type=F32)
            res = (res * factor).astype(BF)
            for cc in range(n_ctx):
                outs[cc, pl.ds(pl.multiple_of(e * ROWS, 16), ROWS), lo:hi] = res[
                    cc * ROWS : (cc + 1) * ROWS
                ]

        @pl.when(e + dn_slots < experts)
        def _():
            dn_copy(e + dn_slots, dslot).start()

        return carry

    lax.fori_loop(0, experts, expert, 0)

    back = others + [c]
    for i, o in enumerate(back):
        for lo in range(0, D, width):
            hi = min(D, lo + width)
            mix[o, lo:hi, :] = lax.dot_general(
                outs[o, :, lo:hi], ptc[o], TN, preferred_element_type=F32
            ).astype(BF)
        for hh in range(2):
            remote(
                mix.at[o, rows_of(quarter(hh, 1 - s))],
                rsib.at[o * 2 + hh],
                c_send.at[i * 2 + hh],
                csib_recv.at[o * 2 + hh],
                sib,
            ).start()

    def wait_sib(o, hh):
        k = o * 2 + hh
        remote(rsib.at[k], rsib.at[k], c_send.at[0], csib_recv.at[k], sib).wait_recv()
        return rsib[k].astype(F32)

    for i, o in enumerate(back):
        mix[o, rows_of(x_j), :] = (
            mix[o, rows_of(x_j), :].astype(F32) + wait_sib(o, 1 - h)
        ).astype(BF)
        remote(mix.at[o, rows_of(x_j)], rx.at[o], c_send.at[8 + i], cx_recv.at[o], xdev).start()
    for i, o in enumerate(back):
        part = mix[o, rows_of(me_j), :].astype(F32) + wait_sib(o, h)
        remote(rx.at[o], rx.at[o], c_send.at[0], cx_recv.at[o], xdev).wait_recv()
        part = part + rx[o].astype(F32)
        if i < n_ctx - 1:
            mix[o, rows_of(me_j), :] = part.astype(BF)
            remote(mix.at[o, rows_of(me_j)], rz.at[c], c_send.at[12 + i], cz_recv.at[c], zdev(o)).start()
        else:
            hidden[...] = hidden[...] + part
    for o in others:
        remote(rz.at[o], rz.at[o], c_send.at[0], cz_recv.at[o], sib).wait_recv()
        hidden[...] = hidden[...] + rz[o].astype(F32)
    out_ref[...] = hidden[...].astype(BF)

    @pl.when(c < n_ctx - 1)
    def _():
        kv_out.wait_send()

    for i in range(n_ctx - 1):
        remote(info.at[c], info.at[c], info_send.at[i], info_recv.at[c], sib).wait_send()
    for i in range(3):
        remote(pa.at[i], ra.at[i], a_send.at[i], a_recv.at[i], sib).wait_send()
    for d in range(3):
        for way, first_o in ((1, c - d), (-1, c + d)):

            @pl.when((c + way >= 0) & (c + way < n_ctx) & (first_o >= 0) & (first_o < n_ctx))
            def _():
                block(me_j, c, d if way > 0 else 3 + d, sib).wait_send()

    for i in range(6, 18):
        block(me_j, c, i, sib).wait_send()
    for i in range(15):
        remote(rx.at[0], rx.at[0], c_send.at[i], cx_recv.at[0], sib).wait_send()


def fused_shards(
    queries,
    keys_values,
    sinks,
    out_weight,
    residual_in,
    norm_gain,
    expert_ids,
    gate_weights,
    gate_up,
    down_weight,
):
    toks = queries.shape[0]
    share = residual_in.shape[1]
    experts = gate_up.shape[0]
    kv_heads = sinks.shape[0] * KV_HEADS // HEADS
    vmem = pl.BlockSpec(memory_space=pltpu.VMEM)
    hbm = pl.BlockSpec(memory_space=pl.ANY)
    gu_slots, dn_slots = min(3, experts), min(2, experts)
    dma = pltpu.SemaphoreType.DMA
    out = pl.pallas_call(
        fused_kernel,
        out_shape=jax.ShapeDtypeStruct((share, toks), BF),
        in_specs=[vmem, vmem, pl.BlockSpec(memory_space=pltpu.SMEM), hbm, vmem, vmem, vmem, vmem, hbm, hbm],
        out_specs=vmem,
        scratch_shapes=[
            pltpu.VMEM((toks, kv_heads * 2 * HD), BF),
            pltpu.VMEM((experts, 4 * ROWS, 4 * toks), BF),
            pltpu.VMEM((experts, 4 * ROWS, 1), F32),
            pltpu.VMEM((toks, kv_heads * 2 * HD), BF),
            pltpu.VMEM((D, out_weight.shape[0]), BF),
            pltpu.VMEM((gu_slots, 2, share, D), BF),
            pltpu.VMEM((dn_slots, share, D), BF),
            pltpu.VMEM(queries.shape, BF),
            pltpu.VMEM((3, share, toks), BF),
            pltpu.VMEM((3, share, toks), BF),
            pltpu.VMEM((share, toks), F32),
            pltpu.VMEM((4, 2 * TOP, toks), F32),
            pltpu.VMEM((16, share + EXTRA, toks), BF),
            pltpu.VMEM((experts, D, 4 * ROWS), BF),
            pltpu.VMEM((share, 4 * ROWS), BF),
            pltpu.VMEM((4, experts * ROWS, D), BF),
            pltpu.VMEM((4, experts * ROWS, toks), BF),
            pltpu.VMEM((4, D, toks), BF),
            pltpu.VMEM((8, share, toks), BF),
            pltpu.VMEM((4, share, toks), BF),
            pltpu.VMEM((4, share, toks), BF),
            dma((1 + gu_slots + dn_slots,)),
            dma((2,)),
            dma((3,)),
            dma((4,)),
            dma((3,)),
            dma((3,)),
            dma((18,)),
            dma((16,)),
            dma((15,)),
            dma((8,)),
            dma((4,)),
            dma((4,)),
        ],
        compiler_params=pltpu.CompilerParams(
            collective_id=0, has_side_effects=True, vmem_limit_bytes=63 * 1024 * 1024
        ),
    )(
        queries,
        keys_values,
        sinks,
        out_weight.T,
        residual_in.T,
        norm_gain.reshape(-1, share),
        expert_ids.T,
        gate_weights.T,
        gate_up.transpose(0, 2, 3, 1),
        down_weight.transpose(0, 2, 1),
    )
    return out.T


def solution(mesh):
    fits = mesh.shape["ctx"] == 4 and mesh.shape["head"] == 2 and mesh.shape["sub"] == 2
    return jax.shard_map(
        fused_shards if fits else shards,
        mesh=mesh,
        in_specs=(
            P(("groups", "ctx"), ("head", "sub")),
            P(("groups", "ctx"), "head", None),
            P(("head", "sub")),
            P(("head", "sub"), None),
            P(("groups", "ctx"), ("head", "sub")),
            P(),
            P(("groups", "ctx"), None),
            P(("groups", "ctx"), None),
            P("ctx", None, None, ("head", "sub")),
            P("ctx", None, ("head", "sub")),
        ),
        out_specs=P(("groups", "ctx"), ("head", "sub")),
        check_vma=False,
    )
```
